32 devices in a mesh: section: 4 (over x, core), expert: 8 (over z, y).
Axes of the slice: x: 2, y: 2, z: 4, core: 2. Of those that a mesh axis runs over, the one named last changes fastest.
Arguments:
- inputs: bfloat16 [4, 256, 2048], P(None, 'expert'), may hold values from -6 to 6
- cotangent: bfloat16 [4, 256, 2048], P(None, 'expert'), may hold values from -6 to 6
- norm_gain: bfloat16 [4, 2048], P('section'), may hold values from 0.25 to 1.75
- w_gate: bfloat16 [4, 8, 2048, 768], P('section', 'expert'), may hold values from -0.125 to 0.125
- w_up: bfloat16 [4, 8, 2048, 768], P('section', 'expert'), may hold values from -0.125 to 0.125
- w_down: bfloat16 [4, 8, 768, 2048], P('section', 'expert'), may hold values from -0.21875 to 0.21875
- route_ids: int32 [4, 4, 256, 2], P('section', None, 'expert'), may hold values from 0 to 7, all different within a row; in each aligned block of 32 rows (0 to 31, 32 to 63, ..., all dimensions but the last counted through in order) at most 16 rows name the same one
- route_weights: float32 [4, 4, 256, 2], P('section', None, 'expert'), may hold values from 0.2 to 1
Outputs:
- layer_outputs: bfloat16 [4, 4, 256, 2048], P('section', None, 'expert')
- input_grads: bfloat16 [4, 4, 256, 2048], P('section', None, 'expert')
The draws below stay inside these ranges and needn't reach their ends.
Inputs may be any that keep to these rules, and one draw needn't show every extreme that they name: `route_ids`: each token names 2 different experts. In each aligned block of 32 rows (one device's tokens of one micro-batch in one layer) no expert is named by more than 16 tokens, and in some blocks an expert is named by exactly 16.
All inputs are finite; a program needn't handle non-finite values.
Results may differ from the reference program's by a relative error of at most 0.04.
Values may be sent and summed in bfloat16 or wider, within the bound.
A program may use at most 64 MiB of HBM per device.

```python
import math
import jax
import jax.numpy as jnp
import numpy as np
from jax import lax

D = 2048
HID = 768
TOP = 2
MICRO = 4
TOK_DEV = 32
LAYERS = 4
EXPERTS = 8
CAP = 16
TOKENS = 256
N_SECTION = 4
N_EXPERT = 8


def shard_levels(rng, dims, shards, smallest, high):
    def one(axis_at, parts):
        steps = jax.random.uniform(jax.random.fold_in(jax.random.fold_in(rng, 6), axis_at), (parts,), jnp.float32, smallest / len(shards), high / len(shards))
        return jnp.repeat(jnp.exp(steps), dims[axis_at] // parts).reshape((-1,) + (1,) * (len(dims) - axis_at - 1))

    level = one(*shards[0])
    for cut in shards[1:]:
        level = level * one(*cut)
    return level


def routed_block(key, own, number, rows, amount, top, limit, lean):
    order = jax.random.permutation(key, amount)
    packed, usual = portions_of(amount, rows * top, limit, lean, True), portions_of(amount, rows * top, limit, lean, False)
    places = jnp.arange(amount)

    def named(sizes, offset_by):
        used = int((sizes > 0).sum())
        fixed = max(1, used // 4)
        moved = fixed + (places - fixed + offset_by * (used - fixed)) % max(1, amount - fixed)
        return jnp.zeros((amount,), jnp.int32).at[order[jnp.where(places < fixed, places, moved)]].set(jnp.asarray(sizes, jnp.int32))

    sizes = jnp.where(number % 4 == 0, named(packed, number // 4), named(usual, number - number // 4 - 1))
    mixed = jax.random.permutation(jax.random.fold_in(own, 3), amount)
    donor, receiver = mixed[0:amount // 2 * 2:2], mixed[1:amount // 2 * 2:2]
    room = jnp.minimum(sizes[donor] - 1, limit - sizes[receiver]) // 2
    room = jnp.where((donor == order[0]) | (receiver == order[0]) | (sizes[receiver] == 0), 0, jnp.maximum(room, 0))
    moved = jax.random.randint(jax.random.fold_in(own, 4), (amount // 2,), 0, 1 << 20) % (room + 1)
    sizes = sizes.at[donor].add(-moved).at[receiver].add(moved)
    items = jnp.searchsorted(jnp.cumsum(sizes), jnp.arange(rows * top), side="right").astype(jnp.int32)
    listing = items.reshape(top, rows).T
    listing = listing[jax.random.permutation(jax.random.fold_in(own, 1), rows)]
    offset_by = jax.random.randint(jax.random.fold_in(own, 2), (rows, 1), 0, top)
    return jnp.take_along_axis(listing, (jnp.arange(top)[None, :] + offset_by) % top, axis=1)


def portions_of(amount, total, limit, lean, full):
    weights = [(1 << 20) // math.isqrt(grade ** lean) + 1 for grade in range(1, amount + 1)]
    largest = limit if full else min(limit, max(-(-total // amount), total * weights[0] // sum(weights)))
    least = 1 if total - largest >= amount - 1 else 0
    holding, rest = [largest] + [least] * (amount - 1), total - largest - least * (amount - 1)
    while rest > 0:
        movable = [i for i in range(1, amount) if holding[i] < largest] or [i for i in range(1, amount) if holding[i] < limit]
        mass, remaining = sum([weights[i] for i in movable]), rest
        for i in movable:
            extra = min(limit - holding[i], max(1, remaining * weights[i] // mass), rest)
            holding[i] = holding[i] + extra
            rest = rest - extra
    return np.array(holding)


def centred(key, extent, scale, bound, shards=(), kind=jnp.bfloat16):
    drawn = scale * jax.random.normal(key, extent, jnp.float32)
    if shards:
        drawn = drawn * shard_levels(key, extent, shards, -0.22, 0.18)
    return jnp.clip(drawn, -bound, bound).astype(kind)


def setup_inputs(seed: int = 0) -> dict:
    key_of = jax.random.split(jax.random.key(seed), 9)
    inputs = centred(key_of[0], (MICRO, TOKENS, D), 1.0, 6.0, ((1, 8),))
    cotangent = centred(key_of[1], (MICRO, TOKENS, D), 1.0, 6.0, ((1, 8),))
    norm_gain = jnp.clip(1.0 + 0.15 * jax.random.normal(key_of[2], (LAYERS, D), jnp.float32), 0.25, 1.75).astype(jnp.bfloat16)
    w_gate = centred(key_of[3], (LAYERS, EXPERTS, D, HID), D ** -0.5, 0.125, ((0, 4), (1, 8)))
    w_up = centred(key_of[4], (LAYERS, EXPERTS, D, HID), D ** -0.5, 0.125, ((0, 4), (1, 8)))
    w_down = centred(key_of[5], (LAYERS, EXPERTS, HID, D), HID ** -0.5, 0.21875, ((0, 4), (1, 8)))
    route_ids_keys = jax.random.split(jax.random.fold_in(key_of[6], 1), LAYERS * MICRO * TOKENS // TOK_DEV)
    route_ids_turns = jax.random.permutation(jax.random.fold_in(key_of[6], 3), LAYERS * MICRO * TOKENS // TOK_DEV)
    route_ids = jax.vmap(lambda own, number: routed_block(jax.random.fold_in(key_of[6], 2), own, number, TOK_DEV, EXPERTS, TOP, CAP, 2))(route_ids_keys, route_ids_turns).reshape((LAYERS, MICRO, TOKENS, TOP))
    route_weights = jnp.clip(0.2 + 0.8 * jax.random.uniform(key_of[7], (LAYERS, MICRO, TOKENS, TOP), jnp.float32) ** shard_levels(key_of[7], (LAYERS, MICRO, TOKENS, TOP), ((0, 4), (2, 8)), -0.2, 0.2), 0.2, 1.0)
    return dict(inputs=inputs, cotangent=cotangent, norm_gain=norm_gain, w_gate=w_gate, w_up=w_up, w_down=w_down, route_ids=route_ids, route_weights=route_weights)


EPS = 1e-06

def norm_forward(act, gain):
    values = act.astype(jnp.float32)
    scale = lax.rsqrt(lax.optimization_barrier(jnp.mean(values * values, axis=-1, keepdims=True)) + EPS)
    normed = (values * scale * gain.astype(jnp.float32)).astype(jnp.bfloat16)
    return (values, scale, normed)

def norm_backward(d_normed, values, scale, gain, upstream):
    scaled = d_normed * gain.astype(jnp.float32)
    inner = lax.optimization_barrier(jnp.mean(scaled * values, axis=-1, keepdims=True))
    return (upstream.astype(jnp.float32) + scale * scaled - values * scale * scale * scale * inner).astype(jnp.bfloat16)

def contract_last(left, right):
    return lax.dot_general(left, right, (((1,), (1,)), ((), ())), preferred_element_type=jnp.float32)

def expert_forward(rows, gate_w, up_w, down_w):
    gate = jnp.dot(rows, gate_w, preferred_element_type=jnp.float32)
    up = jnp.dot(rows, up_w, preferred_element_type=jnp.float32)
    hidden = (jax.nn.silu(gate) * up).astype(jnp.bfloat16)
    out = jnp.dot(hidden, down_w, preferred_element_type=jnp.float32).astype(jnp.bfloat16)
    return (out, gate, up)

def expert_backward(grads, gate, up, gate_w, up_w, down_w):
    d_hidden = contract_last(grads, down_w)
    sig = jax.nn.sigmoid(gate)
    d_gate = (d_hidden * up * sig * (1.0 + gate * (1.0 - sig))).astype(jnp.bfloat16)
    d_up = (d_hidden * gate * sig).astype(jnp.bfloat16)
    return (contract_last(d_gate, gate_w) + contract_last(d_up, up_w)).astype(jnp.bfloat16)

def route_targets(ids):
    sources = N_EXPERT
    flat = ids.reshape(sources, TOK_DEV * TOP)
    picks = (flat[:, :, None] == jnp.arange(EXPERTS, dtype=jnp.int32)[None, None, :]).astype(jnp.int32)
    earlier = jnp.cumsum(picks, axis=1) - picks
    slot = lax.optimization_barrier(jnp.sum(earlier * picks, axis=2))
    block = jnp.arange(sources, dtype=jnp.int32)[:, None] * CAP
    return (flat * (sources * CAP) + block + slot).reshape(-1).astype(jnp.int32)

def reference(inputs, cotangent, norm_gain, w_gate, w_up, w_down, route_ids, route_weights):
    rows_all = EXPERTS * N_EXPERT * CAP
    token_of = (jnp.arange(TOKENS * TOP, dtype=jnp.int32) // TOP).astype(jnp.int32)
    outputs = [[None] * MICRO for layer in range(N_SECTION)]
    grads = [[None] * MICRO for layer in range(N_SECTION)]
    layer_inputs = [[None] * MICRO for layer in range(N_SECTION)]
    for micro in range(MICRO):
        act = inputs[micro]
        for layer in range(N_SECTION):
            layer_inputs[layer][micro] = act
            values, scale, normed = norm_forward(act, norm_gain[layer])
            target = route_targets(route_ids[layer, micro])
            buffer = jnp.zeros((rows_all, D), normed.dtype).at[target].set(normed[token_of])
            buffer = buffer.reshape(EXPERTS, N_EXPERT * CAP, D)
            outs = lax.map(lambda z: expert_forward(z[0], z[1], z[2], z[3])[0], (buffer, w_gate[layer], w_up[layer], w_down[layer]))
            routed = outs.reshape(rows_all, D)[target].astype(jnp.float32).reshape(TOKENS, TOP, D)
            branch = lax.optimization_barrier(jnp.sum(routed * route_weights[layer, micro][:, :, None], axis=1))
            act = (values + branch).astype(jnp.bfloat16)
            outputs[layer][micro] = act
    for micro in range(MICRO):
        upstream = cotangent[micro]
        for layer in range(N_SECTION - 1, -1, -1):
            values, scale, normed = norm_forward(layer_inputs[layer][micro], norm_gain[layer])
            target = route_targets(route_ids[layer, micro])
            buffer = jnp.zeros((rows_all, D), normed.dtype).at[target].set(normed[token_of])
            buffer = buffer.reshape(EXPERTS, N_EXPERT * CAP, D)
            weighted = (route_weights[layer, micro][:, :, None] * upstream.astype(jnp.float32)[:, None, :]).astype(jnp.bfloat16)
            grad_buffer = jnp.zeros((rows_all, D), weighted.dtype).at[target].set(weighted.reshape(TOKENS * TOP, D))
            grad_buffer = grad_buffer.reshape(EXPERTS, N_EXPERT * CAP, D)

            def one_expert(z):
                out, gate, up = expert_forward(z[0], z[2], z[3], z[4])
                return expert_backward(z[1], gate, up, z[2], z[3], z[4])
            back = lax.map(one_expert, (buffer, grad_buffer, w_gate[layer], w_up[layer], w_down[layer]))
            d_normed = back.reshape(rows_all, D)[target].astype(jnp.float32).reshape(TOKENS, TOP, D)
            d_normed = lax.optimization_barrier(jnp.sum(d_normed, axis=1))
            upstream = norm_backward(d_normed, values, scale, norm_gain[layer], upstream)
            grads[layer][micro] = upstream
    layer_outputs = jnp.stack([jnp.stack(row) for row in outputs])
    input_grads = jnp.stack([jnp.stack(row) for row in grads])
    return (layer_outputs, input_grads)
```

```python
import functools

import jax
import jax.numpy as jnp
from jax import lax
from jax.experimental import pallas as pl
from jax.experimental.pallas import tpu as pltpu
from jax.sharding import PartitionSpec as P

EPS = 1e-06


def passed_along(shard, axis, by):
    size = lax.axis_size(axis)
    pairs = [(i, i + by) for i in range(size) if 0 <= i + by < size]
    return lax.ppermute(shard, axis, pairs)


def norm_forward(act, gain):
    values = act.astype(jnp.float32)
    scale = lax.rsqrt(jnp.mean(values * values, axis=-1, keepdims=True) + EPS)
    normed = (values * scale * gain.astype(jnp.float32)).astype(jnp.bfloat16)
    return (values, scale, normed)


def norm_backward(d_normed, values, scale, gain, upstream):
    scaled = d_normed * gain.astype(jnp.float32)
    inner = jnp.mean(scaled * values, axis=-1, keepdims=True)
    return (
        upstream.astype(jnp.float32) + scale * scaled - values * scale * scale * scale * inner
    ).astype(jnp.bfloat16)


def contract_last(left, right):
    return lax.dot_general(
        left, right, (((1,), (1,)), ((), ())), preferred_element_type=jnp.float32
    )


def contract_first(left, right, exact):
    if exact:
        return lax.dot_general(
            left,
            right,
            (((0,), (0,)), ((), ())),
            preferred_element_type=jnp.float32,
            precision=lax.Precision.HIGHEST,
        )
    return lax.dot_general(
        left, right, (((0,), (0,)), ((), ())), preferred_element_type=jnp.float32
    )


def expert_forward(rows, gate_w, up_w, down_w):
    gate = jnp.dot(rows, gate_w, preferred_element_type=jnp.float32)
    up = jnp.dot(rows, up_w, preferred_element_type=jnp.float32)
    hidden = (jax.nn.silu(gate) * up).astype(jnp.bfloat16)
    out = jnp.dot(hidden, down_w, preferred_element_type=jnp.float32).astype(jnp.bfloat16)
    return (out, gate, up)


def expert_backward(grads, gate, up, gate_w, up_w, down_w):
    d_hidden = contract_last(grads, down_w)
    sig = jax.nn.sigmoid(gate)
    d_gate = (d_hidden * up * sig * (1.0 + gate * (1.0 - sig))).astype(jnp.bfloat16)
    d_up = (d_hidden * gate * sig).astype(jnp.bfloat16)
    return (contract_last(d_gate, gate_w) + contract_last(d_up, up_w)).astype(jnp.bfloat16)


def route_tables(ids, weights, experts, capacity):
    micro, rows, top = ids.shape
    flat = ids.reshape(micro, rows * top)
    picks = (flat[:, :, None] == jnp.arange(experts, dtype=jnp.int32)[None, None, :]).astype(
        jnp.int32
    )
    earlier = jnp.cumsum(picks, axis=1) - picks
    slot = jnp.sum(earlier * picks, axis=2)
    target = flat * capacity + slot
    columns = jnp.arange(experts * capacity, dtype=jnp.int32)
    onehot = (target[:, :, None] == columns[None, None, :]).astype(jnp.float32)
    onehot = onehot.reshape(micro, rows, top, experts * capacity)
    dispatch = jnp.swapaxes(jnp.sum(onehot, axis=2), 1, 2).astype(jnp.bfloat16)
    combine = jnp.sum(onehot * weights[:, :, :, None], axis=2)
    return (dispatch, combine)


def shards_padded(inputs, cotangent, norm_gain, w_gate, w_up, w_down, route_ids, route_weights):
    sections = lax.axis_size("section")
    section = lax.axis_index("section")
    experts = lax.axis_size("expert")
    micro, rows, width = inputs.shape
    top = route_ids.shape[3]
    hid = w_gate.shape[3]
    capacity = 2 * rows * top // experts
    slots = experts * capacity
    gain = norm_gain[0]
    gate_w = w_gate[0, 0]
    up_w = w_up[0, 0]
    down_w = w_down[0, 0]
    dispatch, combine = route_tables(route_ids[0], route_weights[0], experts, capacity)

    def forward_layer(act, index, active):
        values, scale, normed = norm_forward(act, gain)
        pick = lax.dynamic_index_in_dim(dispatch, index, 0, keepdims=False)
        mix = lax.dynamic_index_in_dim(combine, index, 0, keepdims=False)
        sending = jnp.dot(pick, normed, preferred_element_type=jnp.float32).astype(jnp.bfloat16)
        received = lax.all_to_all(
            sending.reshape(experts, capacity, width),
            "expert",
            split_axis=0,
            concat_axis=0,
            tiled=True,
        )
        sources, count, dim = received.shape
        flat_rows = received.reshape(sources * count, dim)

        def serve_working(block):
            return expert_forward(block, gate_w, up_w, down_w)

        def serve_resting(block):
            return (
                jnp.zeros_like(block),
                jnp.zeros((block.shape[0], hid), jnp.float32),
                jnp.zeros((block.shape[0], hid), jnp.float32),
            )

        out, gate, up = lax.cond(active, serve_working, serve_resting, flat_rows)
        back = lax.all_to_all(
            out.reshape(sources, count, dim), "expert", split_axis=0, concat_axis=0, tiled=True
        )
        back, gate, up = (back, gate.reshape(sources, count, hid), up.reshape(sources, count, hid))
        branch = jnp.dot(
            mix,
            back.reshape(slots, width).astype(jnp.float32),
            preferred_element_type=jnp.float32,
            precision=lax.Precision.HIGHEST,
        )
        out = (values + branch).astype(jnp.bfloat16)
        return (out, gate.reshape(slots, hid), up.reshape(slots, hid))

    def backward_layer(upstream, act, index, gate, up, active):
        values, scale, normed = norm_forward(act, gain)
        pick = lax.dynamic_index_in_dim(dispatch, index, 0, keepdims=False)
        mix = lax.dynamic_index_in_dim(combine, index, 0, keepdims=False)
        grad_rows = contract_first(mix, upstream.astype(jnp.float32), True).astype(jnp.bfloat16)
        grad_rows = grad_rows.reshape(experts, capacity, width)
        received = lax.all_to_all(grad_rows, "expert", split_axis=0, concat_axis=0, tiled=True)

        def backward_working(block):
            return expert_backward(block, gate, up, gate_w, up_w, down_w)

        def backward_resting(block):
            return jnp.zeros_like(block)

        d_rows = lax.cond(
            active, backward_working, backward_resting, received.reshape(slots, width)
        )
        returned = lax.all_to_all(
            d_rows.reshape(experts, capacity, width),
            "expert",
            split_axis=0,
            concat_axis=0,
            tiled=True,
        )
        d_normed = contract_first(pick, returned.reshape(slots, width), False)
        return norm_backward(d_normed, values, scale, gain, upstream)

    def keep_row(store, value, index, active):
        old = lax.dynamic_index_in_dim(store, index, 0, keepdims=False)
        fresh = jnp.where(active, value, old)
        return lax.dynamic_update_index_in_dim(store, fresh, index, 0)

    def forward_tick(position, state):
        incoming, saved_in, outputs, gates, ups = state
        active = jnp.logical_and(position >= 0, position < micro)
        index = jnp.clip(position, 0, micro - 1)
        first = lax.dynamic_index_in_dim(inputs, index, 0, keepdims=False)
        act = jnp.where(section == 0, first, incoming)
        out, gate, up = forward_layer(act, index, active)
        saved_in = keep_row(saved_in, act, index, active)
        outputs = keep_row(outputs, out, index, active)
        gates = keep_row(gates, gate, index, active)
        ups = keep_row(ups, up, index, active)
        incoming = passed_along(out, "section", 1)
        return (incoming, saved_in, outputs, gates, ups)

    def backward_tick(position, state, saved):
        incoming, grads = state
        saved_in, gates, ups = saved
        active = jnp.logical_and(position >= 0, position < micro)
        index = jnp.clip(position, 0, micro - 1)
        last = lax.dynamic_index_in_dim(cotangent, index, 0, keepdims=False)
        upstream = jnp.where(section == sections - 1, last, incoming)
        act = lax.dynamic_index_in_dim(saved_in, index, 0, keepdims=False)
        gate = lax.dynamic_index_in_dim(gates, index, 0, keepdims=False)
        up = lax.dynamic_index_in_dim(ups, index, 0, keepdims=False)
        grad = backward_layer(upstream, act, index, gate, up, active)
        grads = keep_row(grads, grad, index, active)
        incoming = passed_along(grad, "section", -1)
        return (incoming, grads)

    zero_rows = jnp.zeros((rows, width), jnp.bfloat16)
    zero_store = jnp.zeros((micro, rows, width), jnp.bfloat16)
    zero_hidden = jnp.zeros((micro, slots, hid), jnp.float32)
    forward_state = (zero_rows, zero_store, zero_store, zero_hidden, zero_hidden)
    backward_state = (zero_rows, zero_store)

    def forward_step(step, state):
        return forward_tick(step - section, state)

    forward_state = lax.fori_loop(0, micro + sections - 1, forward_step, forward_state)
    saved = (forward_state[1], forward_state[3], forward_state[4])

    def backward_step(step, state):
        return backward_tick(step - (sections - 1 - section), state, saved)

    backward_state = lax.fori_loop(0, micro + sections - 1, backward_step, backward_state)
    layer_outputs = forward_state[2][None]
    input_grads = backward_state[1][None]
    return (layer_outputs, input_grads)


def route_masks(ids, weights, capacity, slots):
    rows = ids.shape[0]
    column = lax.broadcasted_iota(jnp.int32, (rows, slots), 1)
    expert = column // capacity
    place = (column - expert * capacity).astype(jnp.float32)
    first = ids[:, 0:1] == expert
    second = ids[:, 1:2] == expert
    named = jnp.where(first | second, 1.0, 0.0)
    below = lax.broadcasted_iota(jnp.int32, (rows, rows), 0) > lax.broadcasted_iota(
        jnp.int32, (rows, rows), 1
    )
    earlier = jnp.dot(
        jnp.where(below, 1.0, 0.0).astype(jnp.bfloat16),
        named.astype(jnp.bfloat16),
        preferred_element_type=jnp.float32,
    )
    pick = jnp.where(earlier == place, named, 0.0)
    mix = pick * jnp.where(first, weights[:, 0:1], weights[:, 1:2])
    high = mix.astype(jnp.bfloat16)
    low = (mix - high.astype(jnp.float32)).astype(jnp.bfloat16)
    return (pick.astype(jnp.bfloat16), high, low)


def kernel(
    sections,
    experts,
    capacity,
    x_ref,
    ct_ref,
    gain_ref,
    ids_ref,
    wts_ref,
    wg_hbm,
    wu_hbm,
    wd_hbm,
    out_ref,
    grad_ref,
    wg,
    wu,
    wd,
    act,
    upg,
    send,
    recv,
    gates,
    ups,
    pick_s,
    high_s,
    low_s,
    hid_a,
    hid_b,
    w_sem,
    send_sem,
    recv_sem,
    pass_send,
    pass_recv,
):
    section = lax.axis_index("section")
    me = lax.axis_index("expert")
    last = sections - 1
    micro, rows, width = x_ref.shape
    slots = experts * capacity
    hid = wg.shape[1]
    tile = 256
    bf16, f32 = jnp.bfloat16, jnp.float32

    loads = [
        pltpu.make_async_copy(src, dst, w_sem.at[i])
        for i, (src, dst) in enumerate(((wg_hbm, wg), (wu_hbm, wu), (wd_hbm, wd)))
    ]
    for load in loads:
        load.start()

    barrier = pltpu.get_barrier_semaphore()
    for off in range(1, experts):
        pl.semaphore_signal(
            barrier,
            inc=1,
            device_id=(section, lax.rem(me + off, experts)),
            device_id_type=pl.DeviceIdType.MESH,
        )

    @pl.when(section > 0)
    def _():
        pl.semaphore_signal(
            barrier, inc=1, device_id=(section - 1, me), device_id_type=pl.DeviceIdType.MESH
        )

    @pl.when(section < last)
    def _():
        pl.semaphore_signal(
            barrier, inc=1, device_id=(section + 1, me), device_id_type=pl.DeviceIdType.MESH
        )

    gain = gain_ref[...].astype(f32)

    @pl.when(section == 0)
    def _():
        act[...] = x_ref[...]

    @pl.when(section == last)
    def _():
        upg[...] = ct_ref[...]

    for m in range(micro):
        pick, high, low = route_masks(ids_ref[m], wts_ref[m], capacity, slots)
        pick_s[m] = pick
        high_s[m] = high
        low_s[m] = low

    neighbours = jnp.where(section > 0, 1, 0) + jnp.where(section < last, 1, 0)
    pl.semaphore_wait(barrier, experts - 1 + neighbours)

    def block(index):
        return pl.ds(pl.multiple_of(index * capacity, capacity), capacity)

    def exchange(kind, m):
        for off in range(1, experts):
            peer = lax.rem(me + off, experts)
            pltpu.make_async_remote_copy(
                src_ref=send.at[kind, m, block(peer)],
                dst_ref=recv.at[kind, m, block(me)],
                send_sem=send_sem.at[kind, m],
                recv_sem=recv_sem.at[kind, m],
                device_id=(section, peer),
                device_id_type=pl.DeviceIdType.MESH,
            ).start()
        own = pltpu.make_async_copy(
            send.at[kind, m, block(me)], recv.at[kind, m, block(me)], recv_sem.at[kind, m]
        )
        own.start()

    def arrive(kind, m):
        pltpu.make_async_copy(
            recv.at[kind, m], recv.at[kind, m], recv_sem.at[kind, m]
        ).wait()

    def sent(kind, m):
        part = send.at[kind, m, pl.ds(0, (experts - 1) * capacity)]
        pltpu.make_async_copy(part, part, send_sem.at[kind, m]).wait()

    def pass_on(src, dst, which, m, to):
        return pltpu.make_async_remote_copy(
            src_ref=src.at[m],
            dst_ref=dst.at[m],
            send_sem=pass_send.at[which, m],
            recv_sem=pass_recv.at[which, m],
            device_id=(to, me),
            device_id_type=pl.DeviceIdType.MESH,
        )

    def first_dims(left, right):
        return lax.dot_general(
            left, right, (((0,), (0,)), ((), ())), preferred_element_type=f32
        )

    def normed_parts(m):
        values = act[m].astype(f32)
        scale = lax.rsqrt(jnp.mean(values * values, axis=-1, keepdims=True) + EPS)
        return values, scale

    def forward(m, carry):
        @pl.when(section > 0)
        def _():
            pass_on(out_ref, act, 0, m, section).wait_recv()

        values, scale = normed_parts(m)
        normed = (values * scale * gain).astype(bf16)
        send[0, m] = first_dims(pick_s[m], normed).astype(bf16)
        exchange(0, m)

        @pl.when(m == 0)
        def _():
            for load in loads:
                load.wait()

        arrive(0, m)
        for at in range(0, hid, tile):
            cols = pl.ds(at, tile)
            gate = jnp.dot(recv[0, m], wg[:, cols], preferred_element_type=f32)
            up = jnp.dot(recv[0, m], wu[:, cols], preferred_element_type=f32)
            gates[m, :, cols] = gate
            ups[m, :, cols] = up
            hid_a[:, cols] = (gate * jax.nn.sigmoid(gate) * up).astype(bf16)
        for at in range(0, width, tile):
            cols = pl.ds(at, tile)
            send[1, m, :, cols] = jnp.dot(
                hid_a[...], wd[:, cols], preferred_element_type=f32
            ).astype(bf16)
        exchange(1, m)
        arrive(1, m)
        back = recv[1, m]
        branch = jnp.dot(high_s[m], back, preferred_element_type=f32) + jnp.dot(
            low_s[m], back, preferred_element_type=f32
        )
        out_ref[m] = (act[m].astype(f32) + branch).astype(bf16)

        @pl.when(section < last)
        def _():
            pass_on(out_ref, act, 0, m, section + 1).start()

        return carry

    lax.fori_loop(0, micro, forward, 0)

    def backward(m, carry):
        @pl.when(section < last)
        def _():
            pass_on(grad_ref, upg, 1, m, section).wait_recv()

        dy = upg[m]
        send[2, m] = (first_dims(high_s[m], dy) + first_dims(low_s[m], dy)).astype(bf16)
        exchange(2, m)
        arrive(2, m)
        for at in range(0, hid, tile):
            cols = pl.ds(at, tile)
            d_hidden = contract_last(recv[2, m], wd[cols, :])
            gate = gates[m, :, cols]
            up = ups[m, :, cols]
            sig = jax.nn.sigmoid(gate)
            hid_a[:, cols] = (d_hidden * up * sig * (1.0 + gate * (1.0 - sig))).astype(bf16)
            hid_b[:, cols] = (d_hidden * gate * sig).astype(bf16)
        for at in range(0, width, tile):
            cols = pl.ds(at, tile)
            send[3, m, :, cols] = (
                contract_last(hid_a[...], wg[cols, :]) + contract_last(hid_b[...], wu[cols, :])
            ).astype(bf16)
        exchange(3, m)
        arrive(3, m)
        d_normed = jnp.dot(pick_s[m], recv[3, m], preferred_element_type=f32)
        values, scale = normed_parts(m)
        scaled = d_normed * gain
        inner = jnp.mean(scaled * values, axis=-1, keepdims=True)
        grad_ref[m] = (
            upg[m].astype(f32) + scale * scaled - values * scale * scale * scale * inner
        ).astype(bf16)

        @pl.when(section > 0)
        def _():
            pass_on(grad_ref, upg, 1, m, section - 1).start()

        return carry

    lax.fori_loop(0, micro, backward, 0)

    def finish(m, carry):
        for kind in range(4):
            sent(kind, m)

        @pl.when(section < last)
        def _():
            pass_on(out_ref, act, 0, m, section + 1).wait_send()

        @pl.when(section > 0)
        def _():
            pass_on(grad_ref, upg, 1, m, section - 1).wait_send()

        return carry

    lax.fori_loop(0, micro, finish, 0)


def shards(inputs, cotangent, norm_gain, w_gate, w_up, w_down, route_ids, route_weights):
    sections = lax.axis_size("section")
    experts = lax.axis_size("expert")
    micro, rows, width = inputs.shape
    top = route_ids.shape[3]
    hid = w_gate.shape[3]
    capacity = 2 * rows * top // experts
    slots = experts * capacity
    if capacity % 16:
        return shards_padded(
            inputs, cotangent, norm_gain, w_gate, w_up, w_down, route_ids, route_weights
        )
    bf16, f32 = jnp.bfloat16, jnp.float32
    vmem = pl.BlockSpec(memory_space=pltpu.VMEM)
    anywhere = pl.BlockSpec(memory_space=pl.ANY)
    kinds = 4
    outs = pl.pallas_call(
        functools.partial(kernel, sections, experts, capacity),
        out_shape=(
            jax.ShapeDtypeStruct((micro, rows, width), bf16),
            jax.ShapeDtypeStruct((micro, rows, width), bf16),
        ),
        in_specs=[vmem] * 5 + [anywhere] * 3,
        out_specs=(vmem, vmem),
        scratch_shapes=[
            pltpu.VMEM((width, hid), bf16),
            pltpu.VMEM((width, hid), bf16),
            pltpu.VMEM((hid, width), bf16),
            pltpu.VMEM((micro, rows, width), bf16),
            pltpu.VMEM((micro, rows, width), bf16),
            pltpu.VMEM((kinds, micro, slots, width), bf16),
            pltpu.VMEM((kinds, micro, slots, width), bf16),
            pltpu.VMEM((micro, slots, hid), f32),
            pltpu.VMEM((micro, slots, hid), f32),
            pltpu.VMEM((micro, rows, slots), bf16),
            pltpu.VMEM((micro, rows, slots), bf16),
            pltpu.VMEM((micro, rows, slots), bf16),
            pltpu.VMEM((slots, hid), bf16),
            pltpu.VMEM((slots, hid), bf16),
            pltpu.SemaphoreType.DMA((3,)),
            pltpu.SemaphoreType.DMA((kinds, micro)),
            pltpu.SemaphoreType.DMA((kinds, micro)),
            pltpu.SemaphoreType.DMA((2, micro)),
            pltpu.SemaphoreType.DMA((2, micro)),
        ],
        compiler_params=pltpu.CompilerParams(
            collective_id=0, has_side_effects=True, vmem_limit_bytes=56 * 2**20
        ),
    )(
        inputs,
        cotangent,
        norm_gain,
        route_ids[0],
        route_weights[0],
        w_gate[0, 0],
        w_up[0, 0],
        w_down[0, 0],
    )
    return (outs[0][None], outs[1][None])


def solution(mesh):
    return jax.shard_map(
        shards,
        mesh=mesh,
        in_specs=(
            P(None, "expert", None),
            P(None, "expert", None),
            P("section", None),
            P("section", "expert", None, None),
            P("section", "expert", None, None),
            P("section", "expert", None, None),
            P("section", None, "expert", None),
            P("section", None, "expert", None),
        ),
        out_specs=(P("section", None, "expert", None), P("section", None, "expert", None)),
        check_vma=False,
    )
```

```python
import functools

import jax
import jax.numpy as jnp
from jax import lax
from jax.experimental import pallas as pl
from jax.experimental.pallas import tpu as pltpu
from jax.sharding import PartitionSpec as P

EPS = 1e-06
PARTS = 2


def passed_along(shard, axis, by):
    size = lax.axis_size(axis)
    pairs = [(i, i + by) for i in range(size) if 0 <= i + by < size]
    return lax.ppermute(shard, axis, pairs)


def norm_forward(act, gain):
    values = act.astype(jnp.float32)
    scale = lax.rsqrt(jnp.mean(values * values, axis=-1, keepdims=True) + EPS)
    normed = (values * scale * gain.astype(jnp.float32)).astype(jnp.bfloat16)
    return (values, scale, normed)


def norm_backward(d_normed, values, scale, gain, upstream):
    scaled = d_normed * gain.astype(jnp.float32)
    inner = jnp.mean(scaled * values, axis=-1, keepdims=True)
    return (
        upstream.astype(jnp.float32) + scale * scaled - values * scale * scale * scale * inner
    ).astype(jnp.bfloat16)


def contract_last(left, right):
    return lax.dot_general(
        left, right, (((1,), (1,)), ((), ())), preferred_element_type=jnp.float32
    )


def contract_first(left, right, exact):
    if exact:
        return lax.dot_general(
            left,
            right,
            (((0,), (0,)), ((), ())),
            preferred_element_type=jnp.float32,
            precision=lax.Precision.HIGHEST,
        )
    return lax.dot_general(
        left, right, (((0,), (0,)), ((), ())), preferred_element_type=jnp.float32
    )


def expert_forward(rows, gate_w, up_w, down_w):
    gate = jnp.dot(rows, gate_w, preferred_element_type=jnp.float32)
    up = jnp.dot(rows, up_w, preferred_element_type=jnp.float32)
    hidden = (jax.nn.silu(gate) * up).astype(jnp.bfloat16)
    out = jnp.dot(hidden, down_w, preferred_element_type=jnp.float32).astype(jnp.bfloat16)
    return (out, gate, up)


def expert_backward(grads, gate, up, gate_w, up_w, down_w):
    d_hidden = contract_last(grads, down_w)
    sig = jax.nn.sigmoid(gate)
    d_gate = (d_hidden * up * sig * (1.0 + gate * (1.0 - sig))).astype(jnp.bfloat16)
    d_up = (d_hidden * gate * sig).astype(jnp.bfloat16)
    return (contract_last(d_gate, gate_w) + contract_last(d_up, up_w)).astype(jnp.bfloat16)


def route_tables(ids, weights, experts, capacity):
    micro, rows, top = ids.shape
    flat = ids.reshape(micro, rows * top)
    picks = (flat[:, :, None] == jnp.arange(experts, dtype=jnp.int32)[None, None, :]).astype(
        jnp.int32
    )
    earlier = jnp.cumsum(picks, axis=1) - picks
    slot = jnp.sum(earlier * picks, axis=2)
    target = flat * capacity + slot
    columns = jnp.arange(experts * capacity, dtype=jnp.int32)
    onehot = (target[:, :, None] == columns[None, None, :]).astype(jnp.float32)
    onehot = onehot.reshape(micro, rows, top, experts * capacity)
    dispatch = jnp.swapaxes(jnp.sum(onehot, axis=2), 1, 2).astype(jnp.bfloat16)
    combine = jnp.sum(onehot * weights[:, :, :, None], axis=2)
    return (dispatch, combine)


def shards_padded(inputs, cotangent, norm_gain, w_gate, w_up, w_down, route_ids, route_weights):
    sections = lax.axis_size("section")
    section = lax.axis_index("section")
    experts = lax.axis_size("expert")
    micro, rows, width = inputs.shape
    top = route_ids.shape[3]
    hid = w_gate.shape[3]
    capacity = 2 * rows * top // experts
    slots = experts * capacity
    gain = norm_gain[0]
    gate_w = w_gate[0, 0]
    up_w = w_up[0, 0]
    down_w = w_down[0, 0]
    dispatch, combine = route_tables(route_ids[0], route_weights[0], experts, capacity)

    def forward_layer(act, index, active):
        values, scale, normed = norm_forward(act, gain)
        pick = lax.dynamic_index_in_dim(dispatch, index, 0, keepdims=False)
        mix = lax.dynamic_index_in_dim(combine, index, 0, keepdims=False)
        sending = jnp.dot(pick, normed, preferred_element_type=jnp.float32).astype(jnp.bfloat16)
        received = lax.all_to_all(
            sending.reshape(experts, capacity, width),
            "expert",
            split_axis=0,
            concat_axis=0,
            tiled=True,
        )
        sources, count, dim = received.shape
        flat_rows = received.reshape(sources * count, dim)

        def serve_working(block):
            return expert_forward(block, gate_w, up_w, down_w)

        def serve_resting(block):
            return (
                jnp.zeros_like(block),
                jnp.zeros((block.shape[0], hid), jnp.float32),
                jnp.zeros((block.shape[0], hid), jnp.float32),
            )

        out, gate, up = lax.cond(active, serve_working, serve_resting, flat_rows)
        back = lax.all_to_all(
            out.reshape(sources, count, dim), "expert", split_axis=0, concat_axis=0, tiled=True
        )
        back, gate, up = (back, gate.reshape(sources, count, hid), up.reshape(sources, count, hid))
        branch = jnp.dot(
            mix,
            back.reshape(slots, width).astype(jnp.float32),
            preferred_element_type=jnp.float32,
            precision=lax.Precision.HIGHEST,
        )
        out = (values + branch).astype(jnp.bfloat16)
        return (out, gate.reshape(slots, hid), up.reshape(slots, hid))

    def backward_layer(upstream, act, index, gate, up, active):
        values, scale, normed = norm_forward(act, gain)
        pick = lax.dynamic_index_in_dim(dispatch, index, 0, keepdims=False)
        mix = lax.dynamic_index_in_dim(combine, index, 0, keepdims=False)
        grad_rows = contract_first(mix, upstream.astype(jnp.float32), True).astype(jnp.bfloat16)
        grad_rows = grad_rows.reshape(experts, capacity, width)
        received = lax.all_to_all(grad_rows, "expert", split_axis=0, concat_axis=0, tiled=True)

        def backward_working(block):
            return expert_backward(block, gate, up, gate_w, up_w, down_w)

        def backward_resting(block):
            return jnp.zeros_like(block)

        d_rows = lax.cond(
            active, backward_working, backward_resting, received.reshape(slots, width)
        )
        returned = lax.all_to_all(
            d_rows.reshape(experts, capacity, width),
            "expert",
            split_axis=0,
            concat_axis=0,
            tiled=True,
        )
        d_normed = contract_first(pick, returned.reshape(slots, width), False)
        return norm_backward(d_normed, values, scale, gain, upstream)

    def keep_row(store, value, index, active):
        old = lax.dynamic_index_in_dim(store, index, 0, keepdims=False)
        fresh = jnp.where(active, value, old)
        return lax.dynamic_update_index_in_dim(store, fresh, index, 0)

    def forward_tick(position, state):
        incoming, saved_in, outputs, gates, ups = state
        active = jnp.logical_and(position >= 0, position < micro)
        index = jnp.clip(position, 0, micro - 1)
        first = lax.dynamic_index_in_dim(inputs, index, 0, keepdims=False)
        act = jnp.where(section == 0, first, incoming)
        out, gate, up = forward_layer(act, index, active)
        saved_in = keep_row(saved_in, act, index, active)
        outputs = keep_row(outputs, out, index, active)
        gates = keep_row(gates, gate, index, active)
        ups = keep_row(ups, up, index, active)
        incoming = passed_along(out, "section", 1)
        return (incoming, saved_in, outputs, gates, ups)

    def backward_tick(position, state, saved):
        incoming, grads = state
        saved_in, gates, ups = saved
        active = jnp.logical_and(position >= 0, position < micro)
        index = jnp.clip(position, 0, micro - 1)
        last = lax.dynamic_index_in_dim(cotangent, index, 0, keepdims=False)
        upstream = jnp.where(section == sections - 1, last, incoming)
        act = lax.dynamic_index_in_dim(saved_in, index, 0, keepdims=False)
        gate = lax.dynamic_index_in_dim(gates, index, 0, keepdims=False)
        up = lax.dynamic_index_in_dim(ups, index, 0, keepdims=False)
        grad = backward_layer(upstream, act, index, gate, up, active)
        grads = keep_row(grads, grad, index, active)
        incoming = passed_along(grad, "section", -1)
        return (incoming, grads)

    zero_rows = jnp.zeros((rows, width), jnp.bfloat16)
    zero_store = jnp.zeros((micro, rows, width), jnp.bfloat16)
    zero_hidden = jnp.zeros((micro, slots, hid), jnp.float32)
    forward_state = (zero_rows, zero_store, zero_store, zero_hidden, zero_hidden)
    backward_state = (zero_rows, zero_store)

    def forward_step(step, state):
        return forward_tick(step - section, state)

    forward_state = lax.fori_loop(0, micro + sections - 1, forward_step, forward_state)
    saved = (forward_state[1], forward_state[3], forward_state[4])

    def backward_step(step, state):
        return backward_tick(step - (sections - 1 - section), state, saved)

    backward_state = lax.fori_loop(0, micro + sections - 1, backward_step, backward_state)
    layer_outputs = forward_state[2][None]
    input_grads = backward_state[1][None]
    return (layer_outputs, input_grads)


def route_masks(ids, weights, capacity, slots):
    rows = ids.shape[0]
    column = lax.broadcasted_iota(jnp.int32, (rows, slots), 1)
    expert = column // capacity
    place = (column - expert * capacity).astype(jnp.float32)
    first = ids[:, 0:1] == expert
    second = ids[:, 1:2] == expert
    named = jnp.where(first | second, 1.0, 0.0)
    below = lax.broadcasted_iota(jnp.int32, (rows, rows), 0) > lax.broadcasted_iota(
        jnp.int32, (rows, rows), 1
    )
    earlier = jnp.dot(
        jnp.where(below, 1.0, 0.0).astype(jnp.bfloat16),
        named.astype(jnp.bfloat16),
        preferred_element_type=jnp.float32,
    )
    pick = jnp.where(earlier == place, named, 0.0)
    mix = pick * jnp.where(first, weights[:, 0:1], weights[:, 1:2])
    high = mix.astype(jnp.bfloat16)
    low = (mix - high.astype(jnp.float32)).astype(jnp.bfloat16)
    return (pick.astype(jnp.bfloat16), high, low)


def kernel(
    sections,
    experts,
    capacity,
    x_ref,
    ct_ref,
    gain_ref,
    ids_ref,
    wts_ref,
    wg_hbm,
    wu_hbm,
    wd_hbm,
    out_ref,
    grad_ref,
    wg,
    wu,
    wd,
    act,
    upg,
    send,
    recv,
    gates,
    ups,
    pick_s,
    high_s,
    low_s,
    hid_a,
    hid_b,
    hid_f,
    w_sem,
    send_sem,
    recv_sem,
    pass_send,
    pass_recv,
):
    section = lax.axis_index("section")
    me = lax.axis_index("expert")
    last = sections - 1
    micro, rows, width = x_ref.shape
    slots = experts * capacity
    hid = wg.shape[1]
    tile = 256
    parts = PARTS
    chunk = width // parts
    bf16, f32 = jnp.bfloat16, jnp.float32

    loads = [
        pltpu.make_async_copy(src, dst, w_sem.at[i])
        for i, (src, dst) in enumerate(((wg_hbm, wg), (wu_hbm, wu), (wd_hbm, wd)))
    ]
    for load in loads:
        load.start()

    barrier = pltpu.get_barrier_semaphore()
    for off in range(1, experts):
        pl.semaphore_signal(
            barrier,
            inc=1,
            device_id=(section, lax.rem(me + off, experts)),
            device_id_type=pl.DeviceIdType.MESH,
        )

    @pl.when(section > 0)
    def _():
        pl.semaphore_signal(
            barrier, inc=1, device_id=(section - 1, me), device_id_type=pl.DeviceIdType.MESH
        )

    @pl.when(section < last)
    def _():
        pl.semaphore_signal(
            barrier, inc=1, device_id=(section + 1, me), device_id_type=pl.DeviceIdType.MESH
        )

    gain = gain_ref[...].astype(f32)

    @pl.when(section == 0)
    def _():
        act[...] = x_ref[...]

    @pl.when(section == last)
    def _():
        upg[...] = ct_ref[...]

    for m in range(micro):
        pick, high, low = route_masks(ids_ref[m], wts_ref[m], capacity, slots)
        pick_s[m] = pick
        high_s[m] = high
        low_s[m] = low

    neighbours = jnp.where(section > 0, 1, 0) + jnp.where(section < last, 1, 0)
    pl.semaphore_wait(barrier, experts - 1 + neighbours)

    def block(index):
        return pl.ds(pl.multiple_of(index * capacity, capacity), capacity)

    def span(part):
        return pl.ds(part * chunk, chunk)

    def exchange(kind, m, part):
        cols = span(part)
        for off in range(1, experts):
            peer = lax.rem(me + off, experts)
            pltpu.make_async_remote_copy(
                src_ref=send.at[kind, m, block(peer), cols],
                dst_ref=recv.at[kind, m, block(me), cols],
                send_sem=send_sem.at[kind, m, part],
                recv_sem=recv_sem.at[kind, m, part],
                device_id=(section, peer),
                device_id_type=pl.DeviceIdType.MESH,
            ).start()
        pltpu.make_async_copy(
            send.at[kind, m, block(me), cols],
            recv.at[kind, m, block(me), cols],
            recv_sem.at[kind, m, part],
        ).start()

    def arrive(kind, m, part):
        whole = recv.at[kind, m, pl.ds(0, slots), span(part)]
        pltpu.make_async_copy(whole, whole, recv_sem.at[kind, m, part]).wait()

    def sent(kind, m, part):
        most = send.at[kind, m, pl.ds(0, (experts - 1) * capacity), span(part)]
        pltpu.make_async_copy(most, most, send_sem.at[kind, m, part]).wait()

    def pass_on(src, dst, which, m, part, to):
        return pltpu.make_async_remote_copy(
            src_ref=src.at[m, pl.ds(0, rows), span(part)],
            dst_ref=dst.at[m, pl.ds(0, rows), span(part)],
            send_sem=pass_send.at[which, m, part],
            recv_sem=pass_recv.at[which, m, part],
            device_id=(to, me),
            device_id_type=pl.DeviceIdType.MESH,
        )

    def first_dims(left, right):
        return lax.dot_general(
            left, right, (((0,), (0,)), ((), ())), preferred_element_type=f32
        )

    def normed_parts(m):
        values = act[m].astype(f32)
        scale = lax.rsqrt(jnp.mean(values * values, axis=-1, keepdims=True) + EPS)
        return values, scale

    def forward_send(m):
        @pl.when(section > 0)
        def _():
            for part in range(parts):
                pass_on(out_ref, act, 0, m, part, section).wait_recv()

        values, scale = normed_parts(m)
        normed = (values * scale * gain).astype(bf16)
        for part in range(parts):
            piece = normed[:, part * chunk : (part + 1) * chunk]
            send[0, m, :, span(part)] = first_dims(pick_s[m], piece).astype(bf16)
            exchange(0, m, part)

        @pl.when(m == 0)
        def _():
            for load in loads:
                load.wait()

    def forward_expert(m):
        for part in range(parts):
            arrive(0, m, part)
            for at in range(0, hid, tile):
                cols = pl.ds(at, tile)
                rows_in = recv[0, m, :, span(part)]
                gate = jnp.dot(rows_in, wg[span(part), cols], preferred_element_type=f32)
                up = jnp.dot(rows_in, wu[span(part), cols], preferred_element_type=f32)
                if part > 0:
                    gate = gates[m, :, cols] + gate
                    up = ups[m, :, cols] + up
                gates[m, :, cols] = gate
                ups[m, :, cols] = up
                if part == parts - 1:
                    hid_a[:, cols] = (gate * jax.nn.sigmoid(gate) * up).astype(bf16)
        for part in range(parts):
            for at in range(part * chunk, (part + 1) * chunk, tile):
                cols = pl.ds(at, tile)
                send[1, m, :, cols] = jnp.dot(
                    hid_a[...], wd[:, cols], preferred_element_type=f32
                ).astype(bf16)
            exchange(1, m, part)

    def forward_finish(m):
        for part in range(parts):
            arrive(1, m, part)
            back = recv[1, m, :, span(part)]
            branch = jnp.dot(high_s[m], back, preferred_element_type=f32) + jnp.dot(
                low_s[m], back, preferred_element_type=f32
            )
            out_ref[m, :, span(part)] = (
                act[m, :, span(part)].astype(f32) + branch
            ).astype(bf16)

            @pl.when(section < last)
            def _():
                pass_on(out_ref, act, 0, m, part, section + 1).start()

    def backward_send(m):
        for part in range(parts):

            @pl.when(section < last)
            def _():
                pass_on(grad_ref, upg, 1, m, part, section).wait_recv()

            dy = upg[m, :, span(part)]
            send[2, m, :, span(part)] = (
                first_dims(high_s[m], dy) + first_dims(low_s[m], dy)
            ).astype(bf16)
            exchange(2, m, part)

    def backward_expert(m):
        for part in range(parts):
            arrive(2, m, part)
            for at in range(0, hid, tile):
                cols = pl.ds(at, tile)
                d_hidden = contract_last(recv[2, m, :, span(part)], wd[cols, span(part)])
                if part > 0:
                    d_hidden = hid_f[:, cols] + d_hidden
                if part < parts - 1:
                    hid_f[:, cols] = d_hidden
                else:
                    gate = gates[m, :, cols]
                    up = ups[m, :, cols]
                    sig = jax.nn.sigmoid(gate)
                    hid_a[:, cols] = (
                        d_hidden * up * sig * (1.0 + gate * (1.0 - sig))
                    ).astype(bf16)
                    hid_b[:, cols] = (d_hidden * gate * sig).astype(bf16)
        for part in range(parts):
            for at in range(part * chunk, (part + 1) * chunk, tile):
                cols = pl.ds(at, tile)
                send[3, m, :, cols] = (
                    contract_last(hid_a[...], wg[cols, :])
                    + contract_last(hid_b[...], wu[cols, :])
                ).astype(bf16)
            exchange(3, m, part)

    def backward_finish(m):
        values, scale = normed_parts(m)
        pieces = []
        total = jnp.zeros((rows, 1), f32)
        for part in range(parts):
            arrive(3, m, part)
            d_normed = jnp.dot(
                pick_s[m], recv[3, m, :, span(part)], preferred_element_type=f32
            )
            at, to = part * chunk, (part + 1) * chunk
            scaled = d_normed * gain[:, at:to]
            total = total + jnp.sum(scaled * values[:, at:to], axis=-1, keepdims=True)
            pieces.append(scaled)
        inner = scale * scale * scale * (total / width)
        for part in range(parts):
            at, to = part * chunk, (part + 1) * chunk
            grad_ref[m, :, span(part)] = (
                upg[m, :, span(part)].astype(f32)
                + scale * pieces[part]
                - values[:, at:to] * inner
            ).astype(bf16)

            @pl.when(section > 0)
            def _():
                pass_on(grad_ref, upg, 1, m, part, section - 1).start()

    def tick(step, carry):
        ahead = step - section
        behind = step - (2 * sections - 1 - section)
        runs_ahead = jnp.logical_and(ahead >= 0, ahead < micro)
        runs_behind = jnp.logical_and(behind >= 0, behind < micro)
        fm = jnp.clip(ahead, 0, micro - 1)
        bm = jnp.clip(behind, 0, micro - 1)
        for forward_part, backward_part in (
            (forward_send, backward_send),
            (forward_expert, backward_expert),
            (forward_finish, backward_finish),
        ):
            pl.when(runs_behind)(functools.partial(backward_part, bm))
            pl.when(runs_ahead)(functools.partial(forward_part, fm))
        return carry

    lax.fori_loop(0, micro + 2 * sections - 1, tick, 0)

    def finish(m, carry):
        for part in range(parts):
            for kind in range(4):
                sent(kind, m, part)

            @pl.when(section < last)
            def _():
                pass_on(out_ref, act, 0, m, part, section + 1).wait_send()

            @pl.when(section > 0)
            def _():
                pass_on(grad_ref, upg, 1, m, part, section - 1).wait_send()

        return carry

    lax.fori_loop(0, micro, finish, 0)


def shards(inputs, cotangent, norm_gain, w_gate, w_up, w_down, route_ids, route_weights):
    sections = lax.axis_size("section")
    experts = lax.axis_size("expert")
    micro, rows, width = inputs.shape
    top = route_ids.shape[3]
    hid = w_gate.shape[3]
    capacity = 2 * rows * top // experts
    slots = experts * capacity
    if capacity % 16:
        return shards_padded(
            inputs, cotangent, norm_gain, w_gate, w_up, w_down, route_ids, route_weights
        )
    bf16, f32 = jnp.bfloat16, jnp.float32
    vmem = pl.BlockSpec(memory_space=pltpu.VMEM)
    anywhere = pl.BlockSpec(memory_space=pl.ANY)
    kinds = 4
    outs = pl.pallas_call(
        functools.partial(kernel, sections, experts, capacity),
        out_shape=(
            jax.ShapeDtypeStruct((micro, rows, width), bf16),
            jax.ShapeDtypeStruct((micro, rows, width), bf16),
        ),
        in_specs=[vmem] * 5 + [anywhere] * 3,
        out_specs=(vmem, vmem),
        scratch_shapes=[
            pltpu.VMEM((width, hid), bf16),
            pltpu.VMEM((width, hid), bf16),
            pltpu.VMEM((hid, width), bf16),
            pltpu.VMEM((micro, rows, width), bf16),
            pltpu.VMEM((micro, rows, width), bf16),
            pltpu.VMEM((kinds, micro, slots, width), bf16),
            pltpu.VMEM((kinds, micro, slots, width), bf16),
            pltpu.VMEM((micro, slots, hid), f32),
            pltpu.VMEM((micro, slots, hid), f32),
            pltpu.VMEM((micro, rows, slots), bf16),
            pltpu.VMEM((micro, rows, slots), bf16),
            pltpu.VMEM((micro, rows, slots), bf16),
            pltpu.VMEM((slots, hid), bf16),
            pltpu.VMEM((slots, hid), bf16),
            pltpu.VMEM((slots, hid), f32),
            pltpu.SemaphoreType.DMA((3,)),
            pltpu.SemaphoreType.DMA((kinds, micro, PARTS)),
            pltpu.SemaphoreType.DMA((kinds, micro, PARTS)),
            pltpu.SemaphoreType.DMA((2, micro, PARTS)),
            pltpu.SemaphoreType.DMA((2, micro, PARTS)),
        ],
        compiler_params=pltpu.CompilerParams(
            collective_id=0, has_side_effects=True, vmem_limit_bytes=56 * 2**20
        ),
    )(
        inputs,
        cotangent,
        norm_gain,
        route_ids[0],
        route_weights[0],
        w_gate[0, 0],
        w_up[0, 0],
        w_down[0, 0],
    )
    return (outs[0][None], outs[1][None])


def solution(mesh):
    return jax.shard_map(
        shards,
        mesh=mesh,
        in_specs=(
            P(None, "expert", None),
            P(None, "expert", None),
            P("section", None),
            P("section", "expert", None, None),
            P("section", "expert", None, None),
            P("section", "expert", None, None),
            P("section", None, "expert", None),
            P("section", None, "expert", None),
        ),
        out_specs=(P("section", None, "expert", None), P("section", None, "expert", None)),
        check_vma=False,
    )
```

```python
import functools

import jax
import jax.numpy as jnp
from jax import lax
from jax.experimental import pallas as pl
from jax.experimental.pallas import tpu as pltpu
from jax.sharding import PartitionSpec as P

EPS = 1e-06
PARTS = 2


def passed_along(shard, axis, by):
    size = lax.axis_size(axis)
    pairs = [(i, i + by) for i in range(size) if 0 <= i + by < size]
    return lax.ppermute(shard, axis, pairs)


def norm_forward(act, gain):
    values = act.astype(jnp.float32)
    scale = lax.rsqrt(jnp.mean(values * values, axis=-1, keepdims=True) + EPS)
    normed = (values * scale * gain.astype(jnp.float32)).astype(jnp.bfloat16)
    return (values, scale, normed)


def norm_backward(d_normed, values, scale, gain, upstream):
    scaled = d_normed * gain.astype(jnp.float32)
    inner = jnp.mean(scaled * values, axis=-1, keepdims=True)
    return (
        upstream.astype(jnp.float32) + scale * scaled - values * scale * scale * scale * inner
    ).astype(jnp.bfloat16)


def contract_last(left, right):
    return lax.dot_general(
        left, right, (((1,), (1,)), ((), ())), preferred_element_type=jnp.float32
    )


def contract_first(left, right, exact):
    if exact:
        return lax.dot_general(
            left,
            right,
            (((0,), (0,)), ((), ())),
            preferred_element_type=jnp.float32,
            precision=lax.Precision.HIGHEST,
        )
    return lax.dot_general(
        left, right, (((0,), (0,)), ((), ())), preferred_element_type=jnp.float32
    )


def expert_forward(rows, gate_w, up_w, down_w):
    gate = jnp.dot(rows, gate_w, preferred_element_type=jnp.float32)
    up = jnp.dot(rows, up_w, preferred_element_type=jnp.float32)
    hidden = (jax.nn.silu(gate) * up).astype(jnp.bfloat16)
    out = jnp.dot(hidden, down_w, preferred_element_type=jnp.float32).astype(jnp.bfloat16)
    return (out, gate, up)


def expert_backward(grads, gate, up, gate_w, up_w, down_w):
    d_hidden = contract_last(grads, down_w)
    sig = jax.nn.sigmoid(gate)
    d_gate = (d_hidden * up * sig * (1.0 + gate * (1.0 - sig))).astype(jnp.bfloat16)
    d_up = (d_hidden * gate * sig).astype(jnp.bfloat16)
    return (contract_last(d_gate, gate_w) + contract_last(d_up, up_w)).astype(jnp.bfloat16)


def route_tables(ids, weights, experts, capacity):
    micro, rows, top = ids.shape
    flat = ids.reshape(micro, rows * top)
    picks = (flat[:, :, None] == jnp.arange(experts, dtype=jnp.int32)[None, None, :]).astype(
        jnp.int32
    )
    earlier = jnp.cumsum(picks, axis=1) - picks
    slot = jnp.sum(earlier * picks, axis=2)
    target = flat * capacity + slot
    columns = jnp.arange(experts * capacity, dtype=jnp.int32)
    onehot = (target[:, :, None] == columns[None, None, :]).astype(jnp.float32)
    onehot = onehot.reshape(micro, rows, top, experts * capacity)
    dispatch = jnp.swapaxes(jnp.sum(onehot, axis=2), 1, 2).astype(jnp.bfloat16)
    combine = jnp.sum(onehot * weights[:, :, :, None], axis=2)
    return (dispatch, combine)


def shards_padded(inputs, cotangent, norm_gain, w_gate, w_up, w_down, route_ids, route_weights):
    sections = lax.axis_size("section")
    section = lax.axis_index("section")
    experts = lax.axis_size("expert")
    micro, rows, width = inputs.shape
    top = route_ids.shape[3]
    hid = w_gate.shape[3]
    capacity = 2 * rows * top // experts
    slots = experts * capacity
    gain = norm_gain[0]
    gate_w = w_gate[0, 0]
    up_w = w_up[0, 0]
    down_w = w_down[0, 0]
    dispatch, combine = route_tables(route_ids[0], route_weights[0], experts, capacity)

    def forward_layer(act, index, active):
        values, scale, normed = norm_forward(act, gain)
        pick = lax.dynamic_index_in_dim(dispatch, index, 0, keepdims=False)
        mix = lax.dynamic_index_in_dim(combine, index, 0, keepdims=False)
        sending = jnp.dot(pick, normed, preferred_element_type=jnp.float32).astype(jnp.bfloat16)
        received = lax.all_to_all(
            sending.reshape(experts, capacity, width),
            "expert",
            split_axis=0,
            concat_axis=0,
            tiled=True,
        )
        sources, count, dim = received.shape
        flat_rows = received.reshape(sources * count, dim)

        def serve_working(block):
            return expert_forward(block, gate_w, up_w, down_w)

        def serve_resting(block):
            return (
                jnp.zeros_like(block),
                jnp.zeros((block.shape[0], hid), jnp.float32),
                jnp.zeros((block.shape[0], hid), jnp.float32),
            )

        out, gate, up = lax.cond(active, serve_working, serve_resting, flat_rows)
        back = lax.all_to_all(
            out.reshape(sources, count, dim), "expert", split_axis=0, concat_axis=0, tiled=True
        )
        back, gate, up = (back, gate.reshape(sources, count, hid), up.reshape(sources, count, hid))
        branch = jnp.dot(
            mix,
            back.reshape(slots, width).astype(jnp.float32),
            preferred_element_type=jnp.float32,
            precision=lax.Precision.HIGHEST,
        )
        out = (values + branch).astype(jnp.bfloat16)
        return (out, gate.reshape(slots, hid), up.reshape(slots, hid))

    def backward_layer(upstream, act, index, gate, up, active):
        values, scale, normed = norm_forward(act, gain)
        pick = lax.dynamic_index_in_dim(dispatch, index, 0, keepdims=False)
        mix = lax.dynamic_index_in_dim(combine, index, 0, keepdims=False)
        grad_rows = contract_first(mix, upstream.astype(jnp.float32), True).astype(jnp.bfloat16)
        grad_rows = grad_rows.reshape(experts, capacity, width)
        received = lax.all_to_all(grad_rows, "expert", split_axis=0, concat_axis=0, tiled=True)

        def backward_working(block):
            return expert_backward(block, gate, up, gate_w, up_w, down_w)

        def backward_resting(block):
            return jnp.zeros_like(block)

        d_rows = lax.cond(
            active, backward_working, backward_resting, received.reshape(slots, width)
        )
        returned = lax.all_to_all(
            d_rows.reshape(experts, capacity, width),
            "expert",
            split_axis=0,
            concat_axis=0,
            tiled=True,
        )
        d_normed = contract_first(pick, returned.reshape(slots, width), False)
        return norm_backward(d_normed, values, scale, gain, upstream)

    def keep_row(store, value, index, active):
        old = lax.dynamic_index_in_dim(store, index, 0, keepdims=False)
        fresh = jnp.where(active, value, old)
        return lax.dynamic_update_index_in_dim(store, fresh, index, 0)

    def forward_tick(position, state):
        incoming, saved_in, outputs, gates, ups = state
        active = jnp.logical_and(position >= 0, position < micro)
        index = jnp.clip(position, 0, micro - 1)
        first = lax.dynamic_index_in_dim(inputs, index, 0, keepdims=False)
        act = jnp.where(section == 0, first, incoming)
        out, gate, up = forward_layer(act, index, active)
        saved_in = keep_row(saved_in, act, index, active)
        outputs = keep_row(outputs, out, index, active)
        gates = keep_row(gates, gate, index, active)
        ups = keep_row(ups, up, index, active)
        incoming = passed_along(out, "section", 1)
        return (incoming, saved_in, outputs, gates, ups)

    def backward_tick(position, state, saved):
        incoming, grads = state
        saved_in, gates, ups = saved
        active = jnp.logical_and(position >= 0, position < micro)
        index = jnp.clip(position, 0, micro - 1)
        last = lax.dynamic_index_in_dim(cotangent, index, 0, keepdims=False)
        upstream = jnp.where(section == sections - 1, last, incoming)
        act = lax.dynamic_index_in_dim(saved_in, index, 0, keepdims=False)
        gate = lax.dynamic_index_in_dim(gates, index, 0, keepdims=False)
        up = lax.dynamic_index_in_dim(ups, index, 0, keepdims=False)
        grad = backward_layer(upstream, act, index, gate, up, active)
        grads = keep_row(grads, grad, index, active)
        incoming = passed_along(grad, "section", -1)
        return (incoming, grads)

    zero_rows = jnp.zeros((rows, width), jnp.bfloat16)
    zero_store = jnp.zeros((micro, rows, width), jnp.bfloat16)
    zero_hidden = jnp.zeros((micro, slots, hid), jnp.float32)
    forward_state = (zero_rows, zero_store, zero_store, zero_hidden, zero_hidden)
    backward_state = (zero_rows, zero_store)

    def forward_step(step, state):
        return forward_tick(step - section, state)

    forward_state = lax.fori_loop(0, micro + sections - 1, forward_step, forward_state)
    saved = (forward_state[1], forward_state[3], forward_state[4])

    def backward_step(step, state):
        return backward_tick(step - (sections - 1 - section), state, saved)

    backward_state = lax.fori_loop(0, micro + sections - 1, backward_step, backward_state)
    layer_outputs = forward_state[2][None]
    input_grads = backward_state[1][None]
    return (layer_outputs, input_grads)


def route_masks(ids, weights, capacity, slots):
    rows = ids.shape[0]
    column = lax.broadcasted_iota(jnp.int32, (rows, slots), 1)
    expert = column // capacity
    place = (column - expert * capacity).astype(jnp.float32)
    first = ids[:, 0:1] == expert
    second = ids[:, 1:2] == expert
    named = jnp.where(first | second, 1.0, 0.0)
    below = lax.broadcasted_iota(jnp.int32, (rows, rows), 0) > lax.broadcasted_iota(
        jnp.int32, (rows, rows), 1
    )
    earlier = jnp.dot(
        jnp.where(below, 1.0, 0.0).astype(jnp.bfloat16),
        named.astype(jnp.bfloat16),
        preferred_element_type=jnp.float32,
    )
    pick = jnp.where(earlier == place, named, 0.0)
    mix = pick * jnp.where(first, weights[:, 0:1], weights[:, 1:2])
    high = mix.astype(jnp.bfloat16)
    low = (mix - high.astype(jnp.float32)).astype(jnp.bfloat16)
    return (pick.astype(jnp.bfloat16), high, low)


def kernel(
    sections,
    experts,
    capacity,
    x_ref,
    ct_ref,
    gain_ref,
    ids_ref,
    wts_ref,
    wg_hbm,
    wu_hbm,
    wd_hbm,
    out_ref,
    grad_ref,
    wg,
    wu,
    wd,
    act,
    upg,
    send,
    recv,
    gates,
    ups,
    pick_s,
    high_s,
    low_s,
    hid_a,
    hid_b,
    hid_f,
    w_sem,
    send_sem,
    recv_sem,
    pass_send,
    pass_recv,
):
    section = lax.axis_index("section")
    me = lax.axis_index("expert")
    last = sections - 1
    micro, rows, width = x_ref.shape
    slots = experts * capacity
    hid = wg.shape[1]
    tile = 256
    parts = PARTS
    chunk = width // parts
    bf16, f32 = jnp.bfloat16, jnp.float32

    loads = [
        pltpu.make_async_copy(src, dst, w_sem.at[i])
        for i, (src, dst) in enumerate(((wg_hbm, wg), (wu_hbm, wu), (wd_hbm, wd)))
    ]
    for load in loads:
        load.start()

    barrier = pltpu.get_barrier_semaphore()
    for off in range(1, experts):
        pl.semaphore_signal(
            barrier,
            inc=1,
            device_id=(section, lax.rem(me + off, experts)),
            device_id_type=pl.DeviceIdType.MESH,
        )

    @pl.when(section > 0)
    def _():
        pl.semaphore_signal(
            barrier, inc=1, device_id=(section - 1, me), device_id_type=pl.DeviceIdType.MESH
        )

    @pl.when(section < last)
    def _():
        pl.semaphore_signal(
            barrier, inc=1, device_id=(section + 1, me), device_id_type=pl.DeviceIdType.MESH
        )

    gain = gain_ref[...].astype(f32)

    @pl.when(section == 0)
    def _():
        act[...] = x_ref[...]

    @pl.when(section == last)
    def _():
        upg[...] = ct_ref[...]

    for m in range(micro):
        pick, high, low = route_masks(ids_ref[m], wts_ref[m], capacity, slots)
        pick_s[m] = pick
        high_s[m] = high
        low_s[m] = low

    neighbours = jnp.where(section > 0, 1, 0) + jnp.where(section < last, 1, 0)
    pl.semaphore_wait(barrier, experts - 1 + neighbours)

    def block(index):
        return pl.ds(pl.multiple_of(index * capacity, capacity), capacity)

    def span(part):
        return pl.ds(part * chunk, chunk)

    def exchange(kind, m, part):
        cols = span(part)
        for off in sorted(range(1, experts), key=lambda o: -abs(o - experts // 2)):
            peer = lax.rem(me + off, experts)
            pltpu.make_async_remote_copy(
                src_ref=send.at[kind, m, block(peer), cols],
                dst_ref=recv.at[kind, m, block(me), cols],
                send_sem=send_sem.at[kind, m, part],
                recv_sem=recv_sem.at[kind, m, part],
                device_id=(section, peer),
                device_id_type=pl.DeviceIdType.MESH,
            ).start()
        pltpu.make_async_copy(
            send.at[kind, m, block(me), cols],
            recv.at[kind, m, block(me), cols],
            recv_sem.at[kind, m, part],
        ).start()

    def arrive(kind, m, part):
        whole = recv.at[kind, m, pl.ds(0, slots), span(part)]
        pltpu.make_async_copy(whole, whole, recv_sem.at[kind, m, part]).wait()

    def sent(kind, m, part):
        most = send.at[kind, m, pl.ds(0, (experts - 1) * capacity), span(part)]
        pltpu.make_async_copy(most, most, send_sem.at[kind, m, part]).wait()

    def pass_on(src, dst, which, m, part, to):
        return pltpu.make_async_remote_copy(
            src_ref=src.at[m, pl.ds(0, rows), span(part)],
            dst_ref=dst.at[m, pl.ds(0, rows), span(part)],
            send_sem=pass_send.at[which, m, part],
            recv_sem=pass_recv.at[which, m, part],
            device_id=(to, me),
            device_id_type=pl.DeviceIdType.MESH,
        )

    def first_dims(left, right):
        return lax.dot_general(
            left, right, (((0,), (0,)), ((), ())), preferred_element_type=f32
        )

    def normed_parts(m):
        values = act[m].astype(f32)
        scale = lax.rsqrt(jnp.mean(values * values, axis=-1, keepdims=True) + EPS)
        return values, scale

    def forward_send(m):
        @pl.when(section > 0)
        def _():
            for part in range(parts):
                pass_on(out_ref, act, 0, m, part, section).wait_recv()

        values, scale = normed_parts(m)
        normed = (values * scale * gain).astype(bf16)
        for part in range(parts):
            piece = normed[:, part * chunk : (part + 1) * chunk]
            send[0, m, :, span(part)] = first_dims(pick_s[m], piece).astype(bf16)
            exchange(0, m, part)

        @pl.when(m == 0)
        def _():
            for load in loads:
                load.wait()

    def forward_expert(m):
        for part in range(parts):
            arrive(0, m, part)
            for at in range(0, hid, tile):
                cols = pl.ds(at, tile)
                rows_in = recv[0, m, :, span(part)]
                gate = jnp.dot(rows_in, wg[span(part), cols], preferred_element_type=f32)
                up = jnp.dot(rows_in, wu[span(part), cols], preferred_element_type=f32)
                if part > 0:
                    gate = gates[m, :, cols] + gate
                    up = ups[m, :, cols] + up
                gates[m, :, cols] = gate
                ups[m, :, cols] = up
                if part == parts - 1:
                    hid_a[:, cols] = (gate * jax.nn.sigmoid(gate) * up).astype(bf16)
        for part in range(parts):
            for at in range(part * chunk, (part + 1) * chunk, tile):
                cols = pl.ds(at, tile)
                send[1, m, :, cols] = jnp.dot(
                    hid_a[...], wd[:, cols], preferred_element_type=f32
                ).astype(bf16)
            exchange(1, m, part)

    def forward_finish(m):
        for part in range(parts):
            arrive(1, m, part)
            back = recv[1, m, :, span(part)]
            branch = jnp.dot(high_s[m], back, preferred_element_type=f32) + jnp.dot(
                low_s[m], back, preferred_element_type=f32
            )
            out_ref[m, :, span(part)] = (
                act[m, :, span(part)].astype(f32) + branch
            ).astype(bf16)

            @pl.when(section < last)
            def _():
                pass_on(out_ref, act, 0, m, part, section + 1).start()

    def backward_send(m):
        for part in range(parts):

            @pl.when(section < last)
            def _():
                pass_on(grad_ref, upg, 1, m, part, section).wait_recv()

            dy = upg[m, :, span(part)]
            send[2, m, :, span(part)] = (
                first_dims(high_s[m], dy) + first_dims(low_s[m], dy)
            ).astype(bf16)
            exchange(2, m, part)

    def backward_expert(m):
        for part in range(parts):
            arrive(2, m, part)
            for at in range(0, hid, tile):
                cols = pl.ds(at, tile)
                d_hidden = contract_last(recv[2, m, :, span(part)], wd[cols, span(part)])
                if part > 0:
                    d_hidden = hid_f[:, cols] + d_hidden
                if part < parts - 1:
                    hid_f[:, cols] = d_hidden
                else:
                    gate = gates[m, :, cols]
                    up = ups[m, :, cols]
                    sig = jax.nn.sigmoid(gate)
                    hid_a[:, cols] = (
                        d_hidden * up * sig * (1.0 + gate * (1.0 - sig))
                    ).astype(bf16)
                    hid_b[:, cols] = (d_hidden * gate * sig).astype(bf16)
        for part in range(parts):
            for at in range(part * chunk, (part + 1) * chunk, tile):
                cols = pl.ds(at, tile)
                send[3, m, :, cols] = (
                    contract_last(hid_a[...], wg[cols, :])
                    + contract_last(hid_b[...], wu[cols, :])
                ).astype(bf16)
            exchange(3, m, part)

    def backward_finish(m):
        values, scale = normed_parts(m)
        pieces = []
        total = jnp.zeros((rows, 1), f32)
        for part in range(parts):
            arrive(3, m, part)
            d_normed = jnp.dot(
                pick_s[m], recv[3, m, :, span(part)], preferred_element_type=f32
            )
            at, to = part * chunk, (part + 1) * chunk
            scaled = d_normed * gain[:, at:to]
            total = total + jnp.sum(scaled * values[:, at:to], axis=-1, keepdims=True)
            pieces.append(scaled)
        inner = scale * scale * scale * (total / width)
        for part in range(parts):
            at, to = part * chunk, (part + 1) * chunk
            grad_ref[m, :, span(part)] = (
                upg[m, :, span(part)].astype(f32)
                + scale * pieces[part]
                - values[:, at:to] * inner
            ).astype(bf16)

            @pl.when(section > 0)
            def _():
                pass_on(grad_ref, upg, 1, m, part, section - 1).start()

    def tick(step, carry):
        ahead = step - section
        behind = step - (2 * sections - 1 - section)
        runs_ahead = jnp.logical_and(ahead >= 0, ahead < micro)
        runs_behind = jnp.logical_and(behind >= 0, behind < micro)
        fm = jnp.clip(ahead, 0, micro - 1)
        bm = jnp.clip(behind, 0, micro - 1)
        for forward_part, backward_part in (
            (forward_send, backward_send),
            (forward_expert, backward_expert),
            (forward_finish, backward_finish),
        ):
            pl.when(runs_behind)(functools.partial(backward_part, bm))
            pl.when(runs_ahead)(functools.partial(forward_part, fm))
        return carry

    lax.fori_loop(0, micro + 2 * sections - 1, tick, 0)

    def finish(m, carry):
        for part in range(parts):
            for kind in range(4):
                sent(kind, m, part)

            @pl.when(section < last)
            def _():
                pass_on(out_ref, act, 0, m, part, section + 1).wait_send()

            @pl.when(section > 0)
            def _():
                pass_on(grad_ref, upg, 1, m, part, section - 1).wait_send()

        return carry

    lax.fori_loop(0, micro, finish, 0)


def shards(inputs, cotangent, norm_gain, w_gate, w_up, w_down, route_ids, route_weights):
    sections = lax.axis_size("section")
    experts = lax.axis_size("expert")
    micro, rows, width = inputs.shape
    top = route_ids.shape[3]
    hid = w_gate.shape[3]
    capacity = 2 * rows * top // experts
    slots = experts * capacity
    if capacity % 16:
        return shards_padded(
            inputs, cotangent, norm_gain, w_gate, w_up, w_down, route_ids, route_weights
        )
    bf16, f32 = jnp.bfloat16, jnp.float32
    vmem = pl.BlockSpec(memory_space=pltpu.VMEM)
    anywhere = pl.BlockSpec(memory_space=pl.ANY)
    kinds = 4
    outs = pl.pallas_call(
        functools.partial(kernel, sections, experts, capacity),
        out_shape=(
            jax.ShapeDtypeStruct((micro, rows, width), bf16),
            jax.ShapeDtypeStruct((micro, rows, width), bf16),
        ),
        in_specs=[vmem] * 5 + [anywhere] * 3,
        out_specs=(vmem, vmem),
        scratch_shapes=[
            pltpu.VMEM((width, hid), bf16),
            pltpu.VMEM((width, hid), bf16),
            pltpu.VMEM((hid, width), bf16),
            pltpu.VMEM((micro, rows, width), bf16),
            pltpu.VMEM((micro, rows, width), bf16),
            pltpu.VMEM((kinds, micro, slots, width), bf16),
            pltpu.VMEM((kinds, micro, slots, width), bf16),
            pltpu.VMEM((micro, slots, hid), f32),
            pltpu.VMEM((micro, slots, hid), f32),
            pltpu.VMEM((micro, rows, slots), bf16),
            pltpu.VMEM((micro, rows, slots), bf16),
            pltpu.VMEM((micro, rows, slots), bf16),
            pltpu.VMEM((slots, hid), bf16),
            pltpu.VMEM((slots, hid), bf16),
            pltpu.VMEM((slots, hid), f32),
            pltpu.SemaphoreType.DMA((3,)),
            pltpu.SemaphoreType.DMA((kinds, micro, PARTS)),
            pltpu.SemaphoreType.DMA((kinds, micro, PARTS)),
            pltpu.SemaphoreType.DMA((2, micro, PARTS)),
            pltpu.SemaphoreType.DMA((2, micro, PARTS)),
        ],
        compiler_params=pltpu.CompilerParams(
            collective_id=0, has_side_effects=True, vmem_limit_bytes=56 * 2**20
        ),
    )(
        inputs,
        cotangent,
        norm_gain,
        route_ids[0],
        route_weights[0],
        w_gate[0, 0],
        w_up[0, 0],
        w_down[0, 0],
    )
    return (outs[0][None], outs[1][None])


def solution(mesh):
    return jax.shard_map(
        shards,
        mesh=mesh,
        in_specs=(
            P(None, "expert", None),
            P(None, "expert", None),
            P("section", None),
            P("section", "expert", None, None),
            P("section", "expert", None, None),
            P("section", "expert", None, None),
            P("section", None, "expert", None),
            P("section", None, "expert", None),
        ),
        out_specs=(P("section", None, "expert", None), P("section", None, "expert", None)),
        check_vma=False,
    )
```
